32 devices in a mesh: row: 8 (over y, x, core), col: 4 (over z).
Axes of the slice: x: 2, y: 2, z: 4, core: 2. Of those that a mesh axis runs over, the one named last changes fastest.
Arguments:
- train_grads: bfloat16 [4096, 8192], P('row', 'col'), may hold values from -16 to 16
- query_grads: bfloat16 [2048, 8192], P('col', 'row'), may hold values from -6 to 6
Outputs:
- scores: float32 [4096, 2048], P('row', 'col')
The draws below stay inside these ranges and needn't reach their ends.
All inputs are finite; a program needn't handle non-finite values.
Results may differ from the reference program's by a relative error of at most 0.0081.
Values may be sent and summed in bfloat16 or wider, within the bound.
A program may use at most 128 MiB of HBM per device.

```python
import math
import jax
import jax.numpy as jnp
from jax import lax

PROJ = 64
LAYERS = 2
FEATURES = 8192
TRAIN = 4096
QUERY = 2048


def draw_train_grads(key, part):
    keys = jax.random.split(jax.random.fold_in(key, 71), 5)
    shape = (TRAIN, LAYERS, PROJ, PROJ)
    base = jax.random.truncated_normal(keys[0], -4.0, 4.0, shape, jnp.float32)
    out_scale = jnp.exp(jax.random.uniform(keys[1], (1, LAYERS, PROJ, 1), jnp.float32, 0.0, 2.302585))
    in_scale = jnp.exp(jax.random.uniform(keys[2], (1, LAYERS, 1, PROJ), jnp.float32, 0.0, 2.302585))
    mixing = jnp.eye(PROJ, dtype=jnp.float32) + 0.6 * jax.random.normal(keys[3], (LAYERS, PROJ, PROJ), jnp.float32) / PROJ ** 0.5
    mixed = jnp.einsum('nloi,lij->nloj', base * out_scale, mixing) * in_scale
    ramp = 1.0 + 2.0 * jnp.arange(TRAIN, dtype=jnp.float32) / max(TRAIN - 1, 1)
    jitter = jnp.exp(jax.random.uniform(keys[4], (TRAIN,), jnp.float32, -0.5, 0.5))
    example_scale = (ramp * jitter)[:, None, None, None]
    values = jnp.clip(mixed * example_scale / 30.0, -16.0, 16.0)
    return values.reshape(TRAIN, LAYERS * PROJ * PROJ).astype(jnp.bfloat16)


def steps_of(own_key, dims, cuts, low, high):
    factor_of = 1.0
    for position, shards_of in cuts:
        steps = jax.random.uniform(jax.random.fold_in(jax.random.fold_in(own_key, 6), position), (shards_of,), jnp.float32, low / len(cuts), high / len(cuts))
        factor_of = factor_of * jnp.repeat(jnp.exp(steps), dims[position] // shards_of).reshape((-1,) + (1,) * (len(dims) - 1 - position))
    return factor_of


def noise(key, shape, width, limit, cuts=(), held_as=jnp.bfloat16):
    factor_of = steps_of(key, shape, cuts, -0.22, 0.18) if cuts else 1.0
    drawn = jax.random.normal(key, shape, jnp.float32) * width * factor_of
    return jnp.minimum(jnp.maximum(drawn, -limit), limit).astype(held_as)


def setup_inputs(seed: int = 0) -> dict:
    key_of = jax.random.split(jax.random.key(seed), 3)
    train_grads = draw_train_grads(jax.random.fold_in(key_of[2], 71), 0)
    query_grads = noise(key_of[1], (QUERY, FEATURES), 1.0, 6.0, ((0, 4), (1, 8)))
    return {"train_grads": train_grads, "query_grads": query_grads}


damping_ratio = 0.1

def invert_factors(factors):
    size = factors.shape[-1]
    identity = jnp.eye(size, dtype=jnp.float32)
    trace_value = jnp.trace(factors, axis1=1, axis2=2)
    damped = factors + damping_ratio * (trace_value / size)[:, None, None] * identity
    lower_factor = lax.linalg.cholesky(damped)
    lower_inverse = lax.linalg.triangular_solve(lower_factor, jnp.broadcast_to(identity, damped.shape), left_side=True, lower=True)
    result = jnp.einsum('kji,kjl->kil', lower_inverse, lower_inverse, precision=lax.Precision.HIGHEST)
    return result.astype(jnp.bfloat16)

def precondition(queries, inverses):
    layer_count = inverses.shape[0] // 2
    size = inverses.shape[-1]
    count_rows = queries.shape[0]
    values = queries.astype(jnp.float32).reshape(count_rows, layer_count, size, size)
    input_inverse = inverses[:layer_count].astype(jnp.float32)
    output_inverse = inverses[layer_count:].astype(jnp.float32)
    half = jnp.einsum('nloi,lij->nloj', values, input_inverse, precision=lax.Precision.HIGHEST).astype(jnp.bfloat16)
    result = jnp.einsum('lop,nlpj->nloj', output_inverse, half.astype(jnp.float32), precision=lax.Precision.HIGHEST)
    return result.reshape(count_rows, -1).astype(jnp.bfloat16)

def reference(train_grads, query_grads):
    grads = train_grads.astype(jnp.float32).reshape(TRAIN, LAYERS, PROJ, PROJ)
    input_factor = jnp.einsum('nloi,nloj->lij', grads, grads, precision=lax.Precision.HIGHEST)
    output_factor = jnp.einsum('nloi,nlpi->lop', grads, grads, precision=lax.Precision.HIGHEST)
    factors = jnp.concatenate([input_factor, output_factor], axis=0) / (TRAIN * PROJ)
    inverses = invert_factors(factors)
    conditioned = precondition(query_grads, inverses)
    total = jnp.dot(train_grads.astype(jnp.float32), conditioned.T.astype(jnp.float32), preferred_element_type=jnp.float32)
    return total * (1.0 / math.sqrt(LAYERS * PROJ * PROJ))
```

```python
import functools
import math

import jax
import jax.numpy as jnp
from jax import lax
from jax.experimental import pallas as pl
from jax.experimental.pallas import tpu as pltpu
from jax.sharding import PartitionSpec as P

PROJ = 64
LAYERS = 2
MESH = pl.DeviceIdType.MESH

damping_ratio = 0.1


def factor_terms(block):
    input_side = jnp.einsum("noi,noj->ij", block, block, preferred_element_type=jnp.float32)
    output_side = jnp.einsum("noi,npi->op", block, block, preferred_element_type=jnp.float32)
    return input_side, output_side


def sum_kernel(rows, group, x_ref, out_ref, buf, send_sem, recv_sem):
    row, col = lax.axis_index("row"), lax.axis_index("col")
    first = lax.div(col, group) * group
    index = row * group + lax.rem(col, group)
    count = rows * group

    def peer(step):
        other = lax.rem(index + step, count)
        return lax.div(other, group), first + lax.rem(other, group)

    barrier = pltpu.get_barrier_semaphore()
    for step in range(1, count):
        pl.semaphore_signal(barrier, inc=1, device_id=peer(step), device_id_type=MESH)
    pl.semaphore_wait(barrier, count - 1)
    copies = []
    for step in range(1, count):
        copy = pltpu.make_async_remote_copy(
            src_ref=x_ref,
            dst_ref=buf.at[step - 1],
            send_sem=send_sem.at[step - 1],
            recv_sem=recv_sem.at[step - 1],
            device_id=peer(step),
            device_id_type=MESH,
        )
        copy.start()
        copies.append(copy)
    total = x_ref[...]
    for step in range(1, count):
        copies[step - 1].wait_recv()
        total = total + buf[step - 1]
    out_ref[...] = total
    for copy in copies:
        copy.wait_send()


def sum_over_group(terms, rows, group):
    count = rows * group
    return pl.pallas_call(
        functools.partial(sum_kernel, rows, group),
        out_shape=jax.ShapeDtypeStruct(terms.shape, jnp.float32),
        in_specs=[pl.BlockSpec(memory_space=pltpu.VMEM)],
        out_specs=pl.BlockSpec(memory_space=pltpu.VMEM),
        scratch_shapes=[
            pltpu.VMEM((count - 1,) + terms.shape, jnp.float32),
            pltpu.SemaphoreType.DMA((count - 1,)),
            pltpu.SemaphoreType.DMA((count - 1,)),
        ],
        compiler_params=pltpu.CompilerParams(collective_id=0, has_side_effects=True),
    )(terms)


def invert_kernel(scale, x_ref, out_ref):
    size = PROJ
    across = lax.broadcasted_iota(jnp.int32, (size, size), 1)
    down = lax.broadcasted_iota(jnp.int32, (size, size), 0)
    diagonal = across == down
    states = []
    for side in range(2):
        factor = x_ref[side] * scale
        trace = jnp.sum(jnp.sum(jnp.where(diagonal, factor, 0.0), axis=1, keepdims=True), axis=0, keepdims=True)
        states.append(factor + jnp.where(diagonal, damping_ratio * (trace / size), 0.0))
    for k in range(size):
        for side in range(2):
            value = states[side]
            column = value[:, k : k + 1]
            row = value[k : k + 1, :]
            inverse_pivot = 1.0 / value[k : k + 1, k : k + 1]
            unit_row = jnp.where(across[:1] == k, 1.0, row) * inverse_pivot
            cleared = jnp.where(across == k, 0.0, value)
            updated = cleared - column * unit_row
            states[side] = jnp.where(down == k, unit_row, updated)
    for side in range(2):
        out_ref[side] = states[side].astype(jnp.bfloat16)


def invert(factors, scale):
    return pl.pallas_call(
        functools.partial(invert_kernel, scale),
        out_shape=jax.ShapeDtypeStruct((2, PROJ, PROJ), jnp.bfloat16),
        in_specs=[pl.BlockSpec(memory_space=pltpu.VMEM)],
        out_specs=pl.BlockSpec(memory_space=pltpu.VMEM),
    )(factors)


def picks(parts, order, axis):
    return jnp.concatenate(
        [lax.dynamic_index_in_dim(parts, index, axis, keepdims=False) for index in order], axis=axis
    )


def local(rows, cols, train_grads, query_grads):
    group = cols // LAYERS
    row, col = lax.axis_index("row"), lax.axis_index("col")
    place = lax.rem(col, group)
    layer = lax.div(col, group)
    count, width = train_grads.shape
    part = count // group
    outputs = width // PROJ

    def shifted(value, step):
        pairs = [(c, c // group * group + (c + step) % group) for c in range(cols)]
        return lax.ppermute(value, "col", pairs)

    def chunk(index):
        return lax.dynamic_slice_in_dim(train_grads, lax.rem(index, group) * part, part, 0)

    turns = []
    for k in range(group):
        pieces = [chunk(place + k)]
        for step in range(1, group):
            pieces.append(shifted(chunk(place + step + k), step))
        turns.append(jnp.stack(pieces, axis=1))

    def to_order(value, axis):
        parts = value.reshape(value.shape[:axis] + (group, value.shape[axis] // group) + value.shape[axis + 1 :])
        return picks(parts, [lax.rem(place - t + group, group) for t in range(group)], axis)

    input_side, output_side = factor_terms(turns[0].reshape(part, PROJ, PROJ))
    output_side = to_order(to_order(output_side, 0), 1)
    factors = sum_over_group(jnp.stack([input_side, output_side]), rows, group)
    inverses = invert(factors, 1.0 / (count * rows * PROJ))

    half_rows = rows // LAYERS
    swaps = []
    for r in range(rows):
        for c in range(cols):
            if r // half_rows != c // group:
                source = r * cols + c
                swaps.append((source, (r + half_rows) % rows * cols + (c + group) % cols))
            else:
                swaps.append((r * cols + c, r * cols + c))
    own_query = lax.ppermute(query_grads, ("row", "col"), swaps)
    queries = lax.all_gather(own_query, "row", axis=0)
    query_count, query_width = query_grads.shape
    queries = queries.reshape(LAYERS, half_rows, query_count, query_width)

    examples = jnp.concatenate(turns, axis=0).reshape(count, PROJ, PROJ)
    half = jnp.einsum(
        "noi,ij->noj", examples, inverses[0], preferred_element_type=jnp.float32
    ).astype(jnp.bfloat16)
    conditioned = jnp.einsum(
        "op,npj->noj", to_order(inverses[1], 1), half, preferred_element_type=jnp.float32
    ).astype(jnp.bfloat16)
    conditioned = conditioned.reshape(count, half_rows, query_width)
    product = jnp.einsum(
        "nqf,sqmf->snm", conditioned, queries, preferred_element_type=jnp.float32
    ) * (1.0 / math.sqrt(LAYERS * PROJ * PROJ))
    kept = jnp.where(layer == 0, product[0], product[1])
    given = jnp.where(layer == 0, product[1], product[0]).astype(jnp.bfloat16)
    pairs = [(c, (c + group) % cols) for c in range(cols)]
    result = kept + lax.ppermute(given, "col", pairs).astype(jnp.float32)
    pieces = result.reshape(group, part, query_count)
    return picks(pieces, [lax.rem(t - place + group, group) for t in range(group)], 0)


def solution(mesh):
    placed = (P("row", "col"), P("col", "row"))
    rows, cols = mesh.shape["row"], mesh.shape["col"]
    return jax.shard_map(
        functools.partial(local, rows, cols),
        mesh=mesh,
        in_specs=placed,
        out_specs=P("row", "col"),
        check_vma=False,
    )
```

```python
import functools
import math

import jax
import jax.numpy as jnp
from jax import lax
from jax.experimental import pallas as pl
from jax.experimental.pallas import tpu as pltpu
from jax.sharding import PartitionSpec as P

PROJ = 64
LAYERS = 2
MESH = pl.DeviceIdType.MESH

damping_ratio = 0.1


def factor_terms(block):
    input_side = jnp.einsum("noi,noj->ij", block, block, preferred_element_type=jnp.float32)
    output_side = jnp.einsum("noi,npi->op", block, block, preferred_element_type=jnp.float32)
    return input_side, output_side


def sum_kernel(rows, group, x_ref, out_ref, buf, send_sem, recv_sem):
    row, col = lax.axis_index("row"), lax.axis_index("col")
    first = lax.div(col, group) * group
    index = row * group + lax.rem(col, group)
    count = rows * group

    def peer(step):
        other = lax.rem(index + step, count)
        return lax.div(other, group), first + lax.rem(other, group)

    barrier = pltpu.get_barrier_semaphore()
    for step in range(1, count):
        pl.semaphore_signal(barrier, inc=1, device_id=peer(step), device_id_type=MESH)
    pl.semaphore_wait(barrier, count - 1)
    copies = []
    for step in range(1, count):
        copy = pltpu.make_async_remote_copy(
            src_ref=x_ref,
            dst_ref=buf.at[step - 1],
            send_sem=send_sem.at[step - 1],
            recv_sem=recv_sem.at[step - 1],
            device_id=peer(step),
            device_id_type=MESH,
        )
        copy.start()
        copies.append(copy)
    total = x_ref[...]
    for step in range(1, count):
        copies[step - 1].wait_recv()
        total = total + buf[step - 1]
    out_ref[...] = total
    for copy in copies:
        copy.wait_send()


def sum_over_group(terms, rows, group):
    count = rows * group
    return pl.pallas_call(
        functools.partial(sum_kernel, rows, group),
        out_shape=jax.ShapeDtypeStruct(terms.shape, jnp.float32),
        in_specs=[pl.BlockSpec(memory_space=pltpu.VMEM)],
        out_specs=pl.BlockSpec(memory_space=pltpu.VMEM),
        scratch_shapes=[
            pltpu.VMEM((count - 1,) + terms.shape, jnp.float32),
            pltpu.SemaphoreType.DMA((count - 1,)),
            pltpu.SemaphoreType.DMA((count - 1,)),
        ],
        compiler_params=pltpu.CompilerParams(collective_id=0, has_side_effects=True),
    )(terms)


def invert_kernel(scale, x_ref, out_ref):
    size = PROJ
    across = lax.broadcasted_iota(jnp.int32, (size, size), 1)
    down = lax.broadcasted_iota(jnp.int32, (size, size), 0)
    diagonal = across == down
    states = []
    for side in range(2):
        factor = x_ref[side] * scale
        trace = jnp.sum(jnp.sum(jnp.where(diagonal, factor, 0.0), axis=1, keepdims=True), axis=0, keepdims=True)
        states.append(factor + jnp.where(diagonal, damping_ratio * (trace / size), 0.0))
    for k in range(size):
        for side in range(2):
            value = states[side]
            column = value[:, k : k + 1]
            row = value[k : k + 1, :]
            inverse_pivot = 1.0 / value[k : k + 1, k : k + 1]
            unit_row = jnp.where(across[:1] == k, 1.0, row) * inverse_pivot
            cleared = jnp.where(across == k, 0.0, value)
            updated = cleared - column * unit_row
            states[side] = jnp.where(down == k, unit_row, updated)
    for side in range(2):
        out_ref[side] = states[side].astype(jnp.bfloat16)


def invert(factors, scale):
    return pl.pallas_call(
        functools.partial(invert_kernel, scale),
        out_shape=jax.ShapeDtypeStruct((2, PROJ, PROJ), jnp.bfloat16),
        in_specs=[pl.BlockSpec(memory_space=pltpu.VMEM)],
        out_specs=pl.BlockSpec(memory_space=pltpu.VMEM),
    )(factors)


def picks(parts, order, axis):
    return jnp.concatenate(
        [lax.dynamic_index_in_dim(parts, index, axis, keepdims=False) for index in order], axis=axis
    )


def local(rows, cols, train_grads, query_grads):
    group = cols // LAYERS
    row, col = lax.axis_index("row"), lax.axis_index("col")
    place = lax.rem(col, group)
    layer = lax.div(col, group)
    count, width = train_grads.shape
    part = count // group
    outputs = width // PROJ

    def shifted(value, step):
        pairs = [(c, c // group * group + (c + step) % group) for c in range(cols)]
        return lax.ppermute(value, "col", pairs)

    def across(value, bit):
        return lax.ppermute(value, "row", [(r, r ^ bit) for r in range(rows)])

    def chunk(index):
        return lax.dynamic_slice_in_dim(train_grads, lax.rem(index, group) * part, part, 0)

    turns = []
    ready = None
    for k in range(group):
        pieces = [chunk(place + k)]
        for step in range(1, group):
            sent = chunk(place + step + k)
            if ready is not None:
                sent, _ = lax.optimization_barrier((sent, ready))
            pieces.append(shifted(sent, step))
        if k == 0:
            ready = pieces[-1]
        turns.append(jnp.stack(pieces, axis=1))

    def to_order(value, axis):
        parts = value.reshape(value.shape[:axis] + (group, value.shape[axis] // group) + value.shape[axis + 1 :])
        return picks(parts, [lax.rem(place - t + group, group) for t in range(group)], axis)

    input_side, output_side = factor_terms(turns[0].reshape(part, PROJ, PROJ))
    output_side = to_order(to_order(output_side, 0), 1)
    factors = sum_over_group(jnp.stack([input_side, output_side]), rows, group)
    inverses = invert(factors, 1.0 / (count * rows * PROJ))

    half_rows = rows // LAYERS
    swaps = []
    for r in range(rows):
        for c in range(cols):
            if r // half_rows != c // group:
                source = r * cols + c
                swaps.append((source, (r + half_rows) % rows * cols + (c + group) % cols))
            else:
                swaps.append((r * cols + c, r * cols + c))
    own_query = lax.ppermute(query_grads, ("row", "col"), swaps)
    query_count, query_width = query_grads.shape
    bits = [1 << k for k in range(1, rows.bit_length() - 1)]
    held = []
    for number, piece in enumerate(jnp.split(own_query, 2, axis=0)):
        by_offset = {0: piece}
        near_core = {}
        for bit in (bits if number == 0 else bits[::-1]):
            arrived = {d ^ bit: across(v, bit) for d, v in by_offset.items()}
            by_offset.update(arrived)
        for d, value in by_offset.items():
            near_core[d ^ 1] = across(value, 1)
        by_offset.update(near_core)
        held.append(by_offset)

    scale = 1.0 / math.sqrt(LAYERS * PROJ * PROJ)
    output_inverse = to_order(inverses[1], 1)
    own_side = lax.div(row, half_rows) == layer
    quarter = lax.rem(row, half_rows)
    pairs = [(c, (c + group) % cols) for c in range(cols)]
    results = []
    for turn in turns:
        half = jnp.einsum(
            "noi,ij->noj", turn.reshape(part, PROJ, PROJ), inverses[0], preferred_element_type=jnp.float32
        ).astype(jnp.bfloat16)
        conditioned = jnp.einsum(
            "op,npj->noj", output_inverse, half, preferred_element_type=jnp.float32
        ).astype(jnp.bfloat16)
        conditioned = conditioned.reshape(part, PROJ * PROJ)
        columns = [
            lax.dynamic_slice_in_dim(conditioned, (quarter ^ d) * query_width, query_width, 1)
            for d in range(half_rows)
        ]
        sides = []
        for side in range(LAYERS):
            products = []
            for by_offset in held:
                products.append(
                    sum(
                        lax.dot_general(
                            columns[d],
                            by_offset[side * half_rows + d],
                            (((1,), (1,)), ((), ())),
                            preferred_element_type=jnp.float32,
                        )
                        for d in range(half_rows)
                    )
                )
            sides.append(jnp.concatenate(products, axis=1) * scale)
        kept = jnp.where(own_side, sides[0], sides[1])
        given = jnp.where(own_side, sides[1], sides[0]).astype(jnp.bfloat16)
        results.append(kept + lax.ppermute(given, "col", pairs).astype(jnp.float32))
    pieces = jnp.stack(results)
    return picks(pieces, [lax.rem(t - place + group, group) for t in range(group)], 0)


def solution(mesh):
    placed = (P("row", "col"), P("col", "row"))
    rows, cols = mesh.shape["row"], mesh.shape["col"]
    return jax.shard_map(
        functools.partial(local, rows, cols),
        mesh=mesh,
        in_specs=placed,
        out_specs=P("row", "col"),
        check_vma=False,
    )
```

```python
import functools
import math

import jax
import jax.numpy as jnp
from jax import lax
from jax.experimental import pallas as pl
from jax.experimental.pallas import tpu as pltpu
from jax.sharding import PartitionSpec as P

PROJ = 64
LAYERS = 2
MESH = pl.DeviceIdType.MESH

damping_ratio = 0.1


def factor_terms(block):
    input_side = jnp.einsum("noi,noj->ij", block, block, preferred_element_type=jnp.float32)
    output_side = jnp.einsum("noi,npi->op", block, block, preferred_element_type=jnp.float32)
    return input_side, output_side


def sum_kernel(rows, group, x_ref, out_ref, buf, send_sem, recv_sem):
    row, col = lax.axis_index("row"), lax.axis_index("col")
    first = lax.div(col, group) * group
    index = row * group + lax.rem(col, group)
    count = rows * group

    def peer(step):
        other = lax.rem(index + step, count)
        return lax.div(other, group), first + lax.rem(other, group)

    barrier = pltpu.get_barrier_semaphore()
    for step in range(1, count):
        pl.semaphore_signal(barrier, inc=1, device_id=peer(step), device_id_type=MESH)
    pl.semaphore_wait(barrier, count - 1)
    copies = []
    for step in range(1, count):
        copy = pltpu.make_async_remote_copy(
            src_ref=x_ref,
            dst_ref=buf.at[step - 1],
            send_sem=send_sem.at[step - 1],
            recv_sem=recv_sem.at[step - 1],
            device_id=peer(step),
            device_id_type=MESH,
        )
        copy.start()
        copies.append(copy)
    total = x_ref[...]
    for step in range(1, count):
        copies[step - 1].wait_recv()
        total = total + buf[step - 1]
    out_ref[...] = total
    for copy in copies:
        copy.wait_send()


def sum_over_group(terms, rows, group):
    count = rows * group
    return pl.pallas_call(
        functools.partial(sum_kernel, rows, group),
        out_shape=jax.ShapeDtypeStruct(terms.shape, jnp.float32),
        in_specs=[pl.BlockSpec(memory_space=pltpu.VMEM)],
        out_specs=pl.BlockSpec(memory_space=pltpu.VMEM),
        scratch_shapes=[
            pltpu.VMEM((count - 1,) + terms.shape, jnp.float32),
            pltpu.SemaphoreType.DMA((count - 1,)),
            pltpu.SemaphoreType.DMA((count - 1,)),
        ],
        compiler_params=pltpu.CompilerParams(collective_id=0, has_side_effects=True),
    )(terms)


def invert_kernel(scale, x_ref, out_ref):
    size = PROJ
    across = lax.broadcasted_iota(jnp.int32, (size, size), 1)
    down = lax.broadcasted_iota(jnp.int32, (size, size), 0)
    diagonal = across == down
    states = []
    for side in range(2):
        factor = x_ref[side] * scale
        trace = jnp.sum(jnp.sum(jnp.where(diagonal, factor, 0.0), axis=1, keepdims=True), axis=0, keepdims=True)
        states.append(factor + jnp.where(diagonal, damping_ratio * (trace / size), 0.0))
    for k in range(size):
        for side in range(2):
            value = states[side]
            column = value[:, k : k + 1]
            row = value[k : k + 1, :]
            inverse_pivot = 1.0 / value[k : k + 1, k : k + 1]
            unit_row = jnp.where(across[:1] == k, 1.0, row) * inverse_pivot
            cleared = jnp.where(across == k, 0.0, value)
            updated = cleared - column * unit_row
            states[side] = jnp.where(down == k, unit_row, updated)
    for side in range(2):
        out_ref[side] = states[side].astype(jnp.bfloat16)


def invert(factors, scale):
    return pl.pallas_call(
        functools.partial(invert_kernel, scale),
        out_shape=jax.ShapeDtypeStruct((2, PROJ, PROJ), jnp.bfloat16),
        in_specs=[pl.BlockSpec(memory_space=pltpu.VMEM)],
        out_specs=pl.BlockSpec(memory_space=pltpu.VMEM),
    )(factors)


def picks(parts, order, axis):
    return jnp.concatenate(
        [lax.dynamic_index_in_dim(parts, index, axis, keepdims=False) for index in order], axis=axis
    )


def local(rows, cols, train_grads, query_grads):
    group = cols // LAYERS
    row, col = lax.axis_index("row"), lax.axis_index("col")
    place = lax.rem(col, group)
    layer = lax.div(col, group)
    count, width = train_grads.shape
    part = count // group
    outputs = width // PROJ

    def shifted(value, step):
        pairs = [(c, c // group * group + (c + step) % group) for c in range(cols)]
        return lax.ppermute(value, "col", pairs)

    def across(value, bit):
        return lax.ppermute(value, "row", [(r, r ^ bit) for r in range(rows)])

    def chunk(index):
        return lax.dynamic_slice_in_dim(train_grads, lax.rem(index, group) * part, part, 0)

    turns = []
    ready = None
    for k in range(group):
        pieces = [chunk(place + k)]
        for step in range(1, group):
            sent = chunk(place + step + k)
            if ready is not None:
                sent, _ = lax.optimization_barrier((sent, ready))
            pieces.append(shifted(sent, step))
        if k == 0:
            ready = pieces[-1]
        turns.append(jnp.stack(pieces, axis=1))

    def to_order(value, axis):
        parts = value.reshape(value.shape[:axis] + (group, value.shape[axis] // group) + value.shape[axis + 1 :])
        return picks(parts, [lax.rem(place - t + group, group) for t in range(group)], axis)

    input_side, output_side = factor_terms(turns[0].reshape(part, PROJ, PROJ))
    output_side = to_order(to_order(output_side, 0), 1)
    factors = sum_over_group(jnp.stack([input_side, output_side]), rows, group)
    inverses = invert(factors, 1.0 / (count * rows * PROJ))

    half_rows = rows // LAYERS
    swaps = []
    for r in range(rows):
        for c in range(cols):
            if r // half_rows != c // group:
                source = r * cols + c
                swaps.append((source, (r + half_rows) % rows * cols + (c + group) % cols))
            else:
                swaps.append((r * cols + c, r * cols + c))
    own_query = lax.ppermute(query_grads, ("row", "col"), swaps)
    query_count, query_width = query_grads.shape
    parity = [[r for r in range(rows) if r % 2 == core] for core in range(2)]
    own_query, _ = lax.optimization_barrier((own_query, ready))
    own_core = lax.all_gather(own_query, "row", axis=0, axis_index_groups=parity)
    own_core, inverses = lax.optimization_barrier((own_core, inverses))
    other_core = across(own_core, 1)
    pair_count = half_rows // 2
    held = [v.reshape(LAYERS, pair_count, query_count, query_width) for v in (own_core, other_core)]
    core = lax.rem(row, 2)

    scale = 1.0 / math.sqrt(LAYERS * PROJ * PROJ)
    output_inverse = to_order(inverses[1], 1)
    own_side = layer == 0
    pairs = [(c, (c + group) % cols) for c in range(cols)]
    results = []
    for turn in turns:
        half = jnp.einsum(
            "noi,ij->noj", turn.reshape(part, PROJ, PROJ), inverses[0], preferred_element_type=jnp.float32
        ).astype(jnp.bfloat16)
        conditioned = jnp.einsum(
            "op,npj->noj", output_inverse, half, preferred_element_type=jnp.float32
        ).astype(jnp.bfloat16)
        conditioned = conditioned.reshape(part, PROJ * PROJ)
        by_core = conditioned.reshape(part, pair_count, 2, query_width)
        product = sum(
            jnp.einsum(
                "nqf,sqmf->snm",
                lax.dynamic_index_in_dim(by_core, core ^ e, 2, keepdims=False),
                held[e],
                preferred_element_type=jnp.float32,
            )
            for e in range(2)
        )
        sides = product * scale
        kept = jnp.where(own_side, sides[0], sides[1])
        given = jnp.where(own_side, sides[1], sides[0]).astype(jnp.bfloat16)
        results.append(kept + lax.ppermute(given, "col", pairs).astype(jnp.float32))
    pieces = jnp.stack(results)
    return picks(pieces, [lax.rem(t - place + group, group) for t in range(group)], 0)


def solution(mesh):
    placed = (P("row", "col"), P("col", "row"))
    rows, cols = mesh.shape["row"], mesh.shape["col"]
    return jax.shard_map(
        functools.partial(local, rows, cols),
        mesh=mesh,
        in_specs=placed,
        out_specs=P("row", "col"),
        check_vma=False,
    )
```

```python
import functools
import math

import jax
import jax.numpy as jnp
from jax import lax
from jax.experimental import pallas as pl
from jax.experimental.pallas import tpu as pltpu
from jax.sharding import PartitionSpec as P

PROJ = 64
LAYERS = 2
MESH = pl.DeviceIdType.MESH

damping_ratio = 0.1


def factor_terms(block):
    input_side = jnp.einsum("noi,noj->ij", block, block, preferred_element_type=jnp.float32)
    output_side = jnp.einsum("noi,npi->op", block, block, preferred_element_type=jnp.float32)
    return input_side, output_side


def sum_kernel(rows, group, x_ref, out_ref, buf, send_sem, recv_sem):
    row, col = lax.axis_index("row"), lax.axis_index("col")
    first = lax.div(col, group) * group
    index = row * group + lax.rem(col, group)
    count = rows * group

    def peer(step):
        other = lax.rem(index + step, count)
        return lax.div(other, group), first + lax.rem(other, group)

    barrier = pltpu.get_barrier_semaphore()
    for step in range(1, count):
        pl.semaphore_signal(barrier, inc=1, device_id=peer(step), device_id_type=MESH)
    pl.semaphore_wait(barrier, count - 1)
    copies = []
    for step in range(1, count):
        copy = pltpu.make_async_remote_copy(
            src_ref=x_ref,
            dst_ref=buf.at[step - 1],
            send_sem=send_sem.at[step - 1],
            recv_sem=recv_sem.at[step - 1],
            device_id=peer(step),
            device_id_type=MESH,
        )
        copy.start()
        copies.append(copy)
    total = x_ref[...]
    for step in range(1, count):
        copies[step - 1].wait_recv()
        total = total + buf[step - 1]
    out_ref[...] = total
    for copy in copies:
        copy.wait_send()


def sum_over_group(terms, rows, group):
    count = rows * group
    return pl.pallas_call(
        functools.partial(sum_kernel, rows, group),
        out_shape=jax.ShapeDtypeStruct(terms.shape, jnp.float32),
        in_specs=[pl.BlockSpec(memory_space=pltpu.VMEM)],
        out_specs=pl.BlockSpec(memory_space=pltpu.VMEM),
        scratch_shapes=[
            pltpu.VMEM((count - 1,) + terms.shape, jnp.float32),
            pltpu.SemaphoreType.DMA((count - 1,)),
            pltpu.SemaphoreType.DMA((count - 1,)),
        ],
        compiler_params=pltpu.CompilerParams(collective_id=0, has_side_effects=True),
    )(terms)


def invert_kernel(scale, x_ref, out_ref):
    size = PROJ
    across = lax.broadcasted_iota(jnp.int32, (size, size), 1)
    down = lax.broadcasted_iota(jnp.int32, (size, size), 0)
    diagonal = across == down
    states = []
    for side in range(2):
        factor = x_ref[side] * scale
        trace = jnp.sum(jnp.sum(jnp.where(diagonal, factor, 0.0), axis=1, keepdims=True), axis=0, keepdims=True)
        states.append(factor + jnp.where(diagonal, damping_ratio * (trace / size), 0.0))
    for k in range(size):
        for side in range(2):
            value = states[side]
            column = value[:, k : k + 1]
            row = value[k : k + 1, :]
            inverse_pivot = 1.0 / value[k : k + 1, k : k + 1]
            unit_row = jnp.where(across[:1] == k, 1.0, row) * inverse_pivot
            cleared = jnp.where(across == k, 0.0, value)
            updated = cleared - column * unit_row
            states[side] = jnp.where(down == k, unit_row, updated)
    for side in range(2):
        out_ref[side] = states[side].astype(jnp.bfloat16)


def invert(factors, scale):
    return pl.pallas_call(
        functools.partial(invert_kernel, scale),
        out_shape=jax.ShapeDtypeStruct((2, PROJ, PROJ), jnp.bfloat16),
        in_specs=[pl.BlockSpec(memory_space=pltpu.VMEM)],
        out_specs=pl.BlockSpec(memory_space=pltpu.VMEM),
    )(factors)


def picks(parts, order, axis):
    return jnp.concatenate(
        [lax.dynamic_index_in_dim(parts, index, axis, keepdims=False) for index in order], axis=axis
    )


def local(rows, cols, train_grads, query_grads):
    group = cols // LAYERS
    row, col = lax.axis_index("row"), lax.axis_index("col")
    place = lax.rem(col, group)
    layer = lax.div(col, group)
    count, width = train_grads.shape
    part = count // group
    outputs = width // PROJ

    def shifted(value, step):
        pairs = [(c, c // group * group + (c + step) % group) for c in range(cols)]
        return lax.ppermute(value, "col", pairs)

    def chunk(index):
        return lax.dynamic_slice_in_dim(train_grads, lax.rem(index, group) * part, part, 0)

    turns = []
    for k in range(group):
        pieces = [chunk(place + k)]
        for step in range(1, group):
            sent = chunk(place + step + k)
            pieces.append(shifted(sent, step))
        turns.append(jnp.stack(pieces, axis=1))

    def to_order(value, axis):
        parts = value.reshape(value.shape[:axis] + (group, value.shape[axis] // group) + value.shape[axis + 1 :])
        return picks(parts, [lax.rem(place - t + group, group) for t in range(group)], axis)

    input_side, output_side = factor_terms(turns[0].reshape(part, PROJ, PROJ))
    output_side = to_order(to_order(output_side, 0), 1)
    factors = sum_over_group(jnp.stack([input_side, output_side]), rows, group)
    inverses = invert(factors, 1.0 / (count * rows * PROJ))

    half_rows = rows // LAYERS
    swaps = []
    for r in range(rows):
        for c in range(cols):
            if r // half_rows != c // group:
                source = r * cols + c
                swaps.append((source, (r + half_rows) % rows * cols + (c + group) % cols))
            else:
                swaps.append((r * cols + c, r * cols + c))
    own_query = lax.ppermute(query_grads, ("row", "col"), swaps)
    query_count, query_width = query_grads.shape
    parity = [[r for r in range(rows) if r % 2 == core] for core in range(2)]
    queries = lax.all_gather(own_query, "row", axis=0)
    queries = queries.reshape(LAYERS, half_rows, query_count, query_width)

    scale = 1.0 / math.sqrt(LAYERS * PROJ * PROJ)
    output_inverse = to_order(inverses[1], 1)
    own_side = layer == 0
    pairs = [(c, (c + group) % cols) for c in range(cols)]
    results = []
    for turn in turns:
        half = jnp.einsum(
            "noi,ij->noj", turn.reshape(part, PROJ, PROJ), inverses[0], preferred_element_type=jnp.float32
        ).astype(jnp.bfloat16)
        conditioned = jnp.einsum(
            "op,npj->noj", output_inverse, half, preferred_element_type=jnp.float32
        ).astype(jnp.bfloat16)
        conditioned = conditioned.reshape(part, PROJ * PROJ)
        product = jnp.einsum(
            "nqf,sqmf->snm",
            conditioned.reshape(part, half_rows, query_width),
            queries,
            preferred_element_type=jnp.float32,
        )
        sides = product * scale
        kept = jnp.where(own_side, sides[0], sides[1])
        given = jnp.where(own_side, sides[1], sides[0]).astype(jnp.bfloat16)
        results.append(kept + lax.ppermute(given, "col", pairs).astype(jnp.float32))
    pieces = jnp.stack(results)
    return picks(pieces, [lax.rem(t - place + group, group) for t in range(group)], 0)


def solution(mesh):
    placed = (P("row", "col"), P("col", "row"))
    rows, cols = mesh.shape["row"], mesh.shape["col"]
    return jax.shard_map(
        functools.partial(local, rows, cols),
        mesh=mesh,
        in_specs=placed,
        out_specs=P("row", "col"),
        check_vma=False,
    )
```
